256 devices in a mesh: clip: 16 (over x, z_hi), seq: 16 (over y, z_lo, core).
Axes of the slice: x: 4, y: 4, z: 8 (z_hi: 4, z_lo: 2; z = z_hi * 2 + z_lo), core: 2. Of those that a mesh axis runs over, the one named last changes fastest.
Arguments:
- queries: bfloat16 [16, 2048, 3072], P('clip', 'seq'), may hold values from -6 to 6
- key_states: bfloat16 [16, 2048, 3072], P('clip', 'seq'), may hold values from -6 to 6
- value_states: bfloat16 [16, 2048, 3072], P('clip', 'seq'), may hold values from -6 to 6
- clip_lengths: int32 [16], replicated, may hold values from 512 to 2048, as said below
- tile_masks: int32 [16, 48, 16, 16], P('clip', 'seq'), may hold values from 0 to 1, as said below
Outputs:
- attended: bfloat16 [16, 2048, 3072], P('clip', 'seq')
The draws below stay inside these ranges and needn't reach their ends.
Inputs may be any that keep to these rules, and one draw needn't show every extreme that they name: `clip_lengths`: every clip has at least 512 live tokens; some clip has exactly 2048. `tile_masks`: entries are 0 or 1; the diagonal tiles (i = j) are always 1.
All inputs are finite; a program needn't handle non-finite values.
Results may differ from the reference program's by a relative error of at most 0.0046.
Values may be sent and summed in bfloat16 or wider, within the bound.
No kernel may reach another device: no remote copies, remote signals or barrier semaphores. Data moves between devices by JAX's collectives and lax.ppermute only.
A program may use at most 64 MiB of HBM per device.

```python
import jax
import jax.numpy as jnp
from jax import lax

H = 48
HD = 64
TILE = 128
CLIPS = 16
LMAX = 2048


def draw_queries(key, part):
    key = jax.random.fold_in(key, 3)
    field = jnp.clip(jax.random.normal(key, (CLIPS, LMAX // TILE, TILE, H * HD)), -4.0, 4.0)
    return field.reshape(CLIPS, LMAX, H * HD).astype(jnp.bfloat16)


def draw_key_states(key, part):
    key = jax.random.fold_in(key, 7)
    field = jnp.clip(jax.random.normal(key, (CLIPS, LMAX // TILE, TILE, H * HD)), -4.0, 4.0)
    return field.reshape(CLIPS, LMAX, H * HD).astype(jnp.bfloat16)


def draw_clip_lengths(key, part):
    key = jax.random.fold_in(key, 11)
    length_key, pick_key = jax.random.split(key)
    lengths = jax.random.randint(length_key, (CLIPS,), LMAX // 4, LMAX + 1)
    chosen = jax.random.randint(pick_key, (), 0, CLIPS)
    return jnp.where(jnp.arange(CLIPS) == chosen, LMAX, lengths).astype(jnp.int32)


def draw_tile_masks(key, part):
    key = jax.random.fold_in(key, 13)
    bits_key, density_key = jax.random.split(key)
    tiles = LMAX // TILE
    bits = jax.random.randint(bits_key, (CLIPS, H, tiles, tiles), 0, 8)
    density = jax.random.randint(density_key, (CLIPS, H, 1, 1), 2, 7)
    kept = (bits < density).astype(jnp.int32)
    diagonal = (jnp.arange(tiles)[:, None] == jnp.arange(tiles)[None, :]).astype(jnp.int32)
    return jnp.maximum(kept, diagonal[None, None]).astype(jnp.int32)


def shard_levels(stream_key, dims, pieces, least, high):
    def one(dim, shards_of):
        steps = jax.random.uniform(jax.random.fold_in(jax.random.fold_in(stream_key, 6), dim), (shards_of,), jnp.float32, least / len(pieces), high / len(pieces))
        return jnp.repeat(jnp.exp(steps), dims[dim] // shards_of).reshape((-1,) + (1,) * (len(dims) - dim - 1))

    gain = one(*pieces[0])
    for cut in pieces[1:]:
        gain = gain * one(*cut)
    return gain


def normal_values(own_key, dims, spread, bound, cuts=(), held_as=jnp.bfloat16):
    result = jax.random.normal(own_key, dims, jnp.float32) * spread
    if len(cuts) > 0:
        result = shard_levels(own_key, dims, cuts, -0.22, 0.18) * result
    return jnp.clip(result, min=-bound, max=bound).astype(held_as)


def setup_inputs(seed: int = 0) -> dict:
    key_list = jax.random.split(jax.random.key(seed), 6)
    return {
        "queries": draw_queries(jax.random.fold_in(key_list[5], 71), 0),
        "key_states": draw_key_states(jax.random.fold_in(key_list[5], 71), 0),
        "value_states": normal_values(key_list[2], (CLIPS, LMAX, H * HD), 1.0, 6.0, ((0, 16), (1, 16))),
        "clip_lengths": draw_clip_lengths(jax.random.fold_in(key_list[5], 71), 0),
        "tile_masks": draw_tile_masks(jax.random.fold_in(key_list[5], 71), 0),
    }


def head_output(query_head, key_head, value_head, mask_head, length):
    positions = jnp.arange(LMAX, dtype=jnp.int32)
    tile_index = positions // TILE
    scores = jnp.dot(query_head.astype(jnp.float32), key_head.astype(jnp.float32).T, precision=lax.Precision.HIGHEST) * (HD ** -0.5)
    allowed = (mask_head[tile_index[:, None], tile_index[None, :]] == 1) & (positions[None, :] < length)
    scores = jnp.where(allowed, scores, -1e30)
    top_score = jnp.max(scores, axis=1, keepdims=True)
    weights = jnp.exp(scores - top_score)
    row_sums = jnp.sum(weights, axis=1, keepdims=True)
    rounded = weights.astype(jnp.bfloat16)
    mixed_rows = jnp.dot(rounded.astype(jnp.float32), value_head.astype(jnp.float32), precision=lax.Precision.HIGHEST) / row_sums
    mixed_rows = jnp.where((positions < length)[:, None], mixed_rows, 0.0)
    return mixed_rows.astype(jnp.bfloat16)


def reference(queries, key_states, value_states, clip_lengths, tile_masks):
    def single_head(flat_index):
        clip_index = (flat_index // H).astype(jnp.int32)
        head_index = (flat_index % H).astype(jnp.int32)
        zero = jnp.int32(0)
        column = (head_index * HD).astype(jnp.int32)
        query_head = lax.dynamic_slice(queries, (clip_index, zero, column), (1, LMAX, HD))[0]
        key_head = lax.dynamic_slice(key_states, (clip_index, zero, column), (1, LMAX, HD))[0]
        value_head = lax.dynamic_slice(value_states, (clip_index, zero, column), (1, LMAX, HD))[0]
        mask_head = tile_masks[clip_index, head_index]
        return head_output(query_head, key_head, value_head, mask_head, clip_lengths[clip_index])

    results = lax.map(single_head, jnp.arange(CLIPS * H, dtype=jnp.int32))
    results = results.reshape(CLIPS, H, LMAX, HD).transpose(0, 2, 1, 3)
    return results.reshape(CLIPS, LMAX, H * HD)
```

```python
import jax
import jax.numpy as jnp
from jax import lax
from jax.experimental import pallas as pl
from jax.experimental.pallas import tpu as pltpu
from jax.sharding import PartitionSpec as P

TILE = 128
SEQ = 16
CHIPS = 8
PAIR = 128
PAIRS = 3
QB = 256
CK = 256
NQ = CHIPS * TILE
NK = 2 * NQ
MASKED = -1e30
SCALE = 0.125 * 1.4426950408889634

ALL_CHIPS = [[2 * chip + core for chip in range(CHIPS)] for core in range(2)]
OTHER_CORE = [(device, device ^ 1) for device in range(SEQ)]


def matmul(a, b, dims):
    return lax.dot_general(a, b, (dims, ((), ())), preferred_element_type=jnp.float32)


def attend(core_ref, length_ref, q_ref, k_own, v_own, k_sib, v_sib, mask_ref, o_ref,
           key_aux, keys, values_t, scores_a, scores_b):
    core = core_ref[0]
    length = length_ref[0]
    lane = lax.broadcasted_iota(jnp.int32, (1, PAIR), 1)
    low = lane < 64
    scores = (scores_a, scores_b)

    @pl.when(pl.program_id(0) == 0)
    def _():
        column = lax.broadcasted_iota(jnp.int32, (TILE, PAIR), 1) & 63
        inside = lax.broadcasted_iota(jnp.int32, (TILE, PAIR), 0)
        for part in range(2):
            parity = core if part == 0 else 1 - core
            for chip in range(CHIPS):
                tile = 2 * chip + parity
                dead = jnp.where(tile * TILE + inside >= length, 16, -1)
                hot = (column == tile) | (column == dead)
                first = part * NQ + chip * TILE
                key_aux[first : first + TILE, :] = hot.astype(jnp.float32).astype(jnp.bfloat16)

    for part, (k_ref, v_ref) in enumerate(((k_own, v_own), (k_sib, v_sib))):
        for chip in range(CHIPS):
            rows = slice(part * NQ + chip * TILE, part * NQ + (chip + 1) * TILE)
            k = k_ref[chip, 0]
            keys[0, rows, :] = jnp.where(low, k, key_aux[rows, :])
            keys[1, rows, :] = jnp.where(low, key_aux[rows, :], k)
            values_t[:, rows] = v_ref[chip, 0].T

    def load_queries(block, head):
        parts = []
        for half in range(2):
            chip = 2 * block + half
            kept = mask_ref[head, pl.ds(2 * chip + core, 1), :]
            bias = jnp.where(kept == 1, 0.0, MASKED)
            bias = jnp.where((lane & 63) < 16, bias, jnp.where((lane & 63) == 16, MASKED, 0.0))
            bias = jnp.broadcast_to(bias, (TILE, PAIR)).astype(jnp.bfloat16)
            q = q_ref[chip, 0]
            parts.append(jnp.where(low, q, bias) if head == 0 else jnp.where(low, bias, q))
        return jnp.concatenate(parts, axis=0)

    def score_chunk(chunk, queries, head, top):
        rows = slice(chunk * CK, (chunk + 1) * CK)
        s = matmul(keys[head, rows, :], queries, ((1,), (1,)))
        scores[head][rows, :] = s
        return jnp.maximum(top, jnp.max(s.reshape(CK // 8, 8, QB), axis=0))

    empty = jnp.full((8, QB), -3e38, jnp.float32)

    def step(block, head, top, next_block):
        queries = load_queries(next_block, 1 - head)
        next_top = empty
        total = jnp.zeros((8, QB), jnp.float32)
        mixed = jnp.zeros((64, QB), jnp.float32)
        row_top = jnp.max(top, axis=0, keepdims=True)
        for chunk in range(NK // CK):
            next_top = score_chunk(chunk, queries, 1 - head, next_top)
            rows = slice(chunk * CK, (chunk + 1) * CK)
            weights = jnp.exp2((scores[head][rows, :] - row_top) * SCALE)
            total = total + jnp.sum(weights.reshape(CK // 8, 8, QB), axis=0)
            mixed = mixed + matmul(
                values_t[64 * head : 64 * head + 64, rows], weights.astype(jnp.bfloat16), ((1,), (0,))
            )
        return next_top, mixed / jnp.sum(total, axis=0, keepdims=True)

    top = empty
    queries = load_queries(0, 0)
    for chunk in range(NK // CK):
        top = score_chunk(chunk, queries, 0, top)

    blocks = NQ // QB
    query = lax.broadcasted_iota(jnp.int32, (1, QB), 1)

    def body(block, top):
        top, first = step(block, 0, top, block)
        top, second = step(block, 1, top, jnp.minimum(block + 1, blocks - 1))
        chip = 2 * block + query // TILE
        live = (2 * chip + core) * TILE + query % TILE < length
        both = jnp.where(live, jnp.concatenate([first, second], axis=0), 0.0).T.astype(jnp.bfloat16)
        o_ref[2 * block] = both[:TILE]
        o_ref[2 * block + 1] = both[TILE:]
        return top

    lax.fori_loop(0, blocks, body, top)


def attention(core, length, own, sibling, masks):
    def tokens(which):
        return pl.BlockSpec((CHIPS, 1, TILE, PAIR), lambda pair: (0, which, 0, pair))

    return pl.pallas_call(
        attend,
        grid=(PAIRS,),
        out_shape=jax.ShapeDtypeStruct((CHIPS, TILE, PAIRS * PAIR), jnp.bfloat16),
        in_specs=[
            pl.BlockSpec(memory_space=pltpu.SMEM),
            pl.BlockSpec(memory_space=pltpu.SMEM),
            tokens(0), tokens(1), tokens(2), tokens(1), tokens(2),
            pl.BlockSpec((2, 16, PAIR), lambda pair: (pair, 0, 0)),
        ],
        out_specs=pl.BlockSpec((CHIPS, TILE, PAIR), lambda pair: (0, 0, pair)),
        scratch_shapes=[
            pltpu.VMEM((NK, PAIR), jnp.bfloat16),
            pltpu.VMEM((2, NK, PAIR), jnp.bfloat16),
            pltpu.VMEM((PAIR, NK), jnp.bfloat16),
            pltpu.VMEM((NK, QB), jnp.float32),
            pltpu.VMEM((NK, QB), jnp.float32),
        ],
        compiler_params=pltpu.CompilerParams(vmem_limit_bytes=40 * 2**20),
        cost_estimate=pl.CostEstimate(
            flops=4 * 6 * NQ * NK * 64, bytes_accessed=8 * 2**20, transcendentals=6 * NQ * NK
        ),
    )(core, length, own, own, own, sibling, sibling, masks)


def split_columns(*refs):
    *arrays, packed, done = refs
    copies = []
    for chip in range(CHIPS):
        for which, array in enumerate(arrays):
            columns = array.at[0, :, pl.ds(chip * PAIRS * PAIR, PAIRS * PAIR)]
            copies.append(pltpu.make_async_copy(columns, packed.at[chip, which], done.at[len(copies)]))
    for copy in copies:
        copy.start()
    for copy in copies:
        copy.wait()


def join_columns(blocks, rows, done):
    copies = [
        pltpu.make_async_copy(
            blocks.at[chip], rows.at[0, :, pl.ds(chip * PAIRS * PAIR, PAIRS * PAIR)], done.at[chip]
        )
        for chip in range(CHIPS)
    ]
    for copy in copies:
        copy.start()
    for copy in copies:
        copy.wait()


def move(kernel, shape, copies, *arrays):
    whole = pl.BlockSpec(memory_space=pl.ANY)
    return pl.pallas_call(
        kernel,
        out_shape=jax.ShapeDtypeStruct(shape, jnp.bfloat16),
        in_specs=[whole] * len(arrays),
        out_specs=whole,
        scratch_shapes=[pltpu.SemaphoreType.DMA((copies,))],
    )(*arrays)


def on_device(queries, key_states, value_states, clip_lengths, tile_masks):
    place = lax.axis_index("seq")
    core = place % 2
    length = lax.dynamic_slice_in_dim(clip_lengths, lax.axis_index("clip"), 1, 0)

    mine = jnp.pad(tile_masks[0], ((0, 0), (0, 0), (0, 48)))
    mine = jnp.concatenate([mine, mine], axis=-1)
    other = lax.ppermute(mine, "seq", OTHER_CORE)
    masks = jnp.where(core == 0, jnp.concatenate([mine, other]), jnp.concatenate([other, mine]))

    packed = move(
        split_columns, (CHIPS, 3, TILE, PAIRS * PAIR), 3 * CHIPS, queries, key_states, value_states
    )
    own = lax.all_to_all(packed, "seq", 0, 0, tiled=True, axis_index_groups=ALL_CHIPS)
    sibling = lax.ppermute(own, "seq", OTHER_CORE)
    mixed = attention(core.reshape(1), length, own, sibling, masks)
    back = lax.all_to_all(mixed, "seq", 0, 0, tiled=True, axis_index_groups=ALL_CHIPS)
    return move(join_columns, (1, TILE, CHIPS * PAIRS * PAIR), CHIPS, back)


def solution(mesh):
    split = P("clip", "seq", None)
    return jax.shard_map(
        on_device,
        mesh=mesh,
        in_specs=(split, split, split, P(), P("clip", "seq", None, None)),
        out_specs=split,
        check_vma=False,
    )
```

```python
import jax
import jax.numpy as jnp
from jax import lax
from jax.experimental import pallas as pl
from jax.experimental.pallas import tpu as pltpu
from jax.sharding import PartitionSpec as P

TILE = 128
SEQ = 16
CHIPS = 8
PAIR = 128
PAIRS = 3
QB = 256
CK = 256
NQ = CHIPS * TILE
NK = 2 * NQ
MASKED = -1e30
SCALE = 0.125 * 1.4426950408889634

ALL_CHIPS = [[2 * chip + core for chip in range(CHIPS)] for core in range(2)]
OTHER_CORE = [(device, device ^ 1) for device in range(SEQ)]


def matmul(a, b, dims):
    return lax.dot_general(a, b, (dims, ((), ())), preferred_element_type=jnp.float32)


def attend(core_ref, length_ref, q_ref, k_own, v_own, k_sib, v_sib, mask_ref, o_ref,
           key_aux, keys, values_t, scores_a, scores_b):
    core = core_ref[0]
    length = length_ref[0]
    lane = lax.broadcasted_iota(jnp.int32, (1, PAIR), 1)
    low = lane < 64
    scores = (scores_a, scores_b)

    @pl.when(pl.program_id(0) == 0)
    def _():
        column = lax.broadcasted_iota(jnp.int32, (TILE, PAIR), 1) & 63
        inside = lax.broadcasted_iota(jnp.int32, (TILE, PAIR), 0)
        for part in range(2):
            parity = core if part == 0 else 1 - core
            for chip in range(CHIPS):
                tile = 2 * chip + parity
                dead = jnp.where(tile * TILE + inside >= length, 16, -1)
                hot = (column == tile) | (column == dead)
                first = part * NQ + chip * TILE
                key_aux[first : first + TILE, :] = hot.astype(jnp.float32).astype(jnp.bfloat16)

    for part, (k_ref, v_ref) in enumerate(((k_own, v_own), (k_sib, v_sib))):
        for chip in range(CHIPS):
            rows = slice(part * NQ + chip * TILE, part * NQ + (chip + 1) * TILE)
            k = k_ref[chip, 0]
            keys[0, rows, :] = jnp.where(low, k, key_aux[rows, :])
            keys[1, rows, :] = jnp.where(low, key_aux[rows, :], k)
            values_t[:, rows] = v_ref[chip, 0].T

    def load_queries(block, head):
        parts = []
        for half in range(2):
            chip = 2 * block + half
            kept = mask_ref[head, pl.ds(2 * chip + core, 1), :]
            bias = jnp.where(kept == 1, 0.0, MASKED)
            bias = jnp.where((lane & 63) < 16, bias, jnp.where((lane & 63) == 16, MASKED, 0.0))
            bias = jnp.broadcast_to(bias, (TILE, PAIR)).astype(jnp.bfloat16)
            q = q_ref[chip, 0]
            parts.append(jnp.where(low, q, bias) if head == 0 else jnp.where(low, bias, q))
        return jnp.concatenate(parts, axis=0)

    def score_chunk(chunk, queries, head, top):
        rows = slice(chunk * CK, (chunk + 1) * CK)
        s = matmul(keys[head, rows, :], queries, ((1,), (1,)))
        scores[head][rows, :] = s
        return jnp.maximum(top, jnp.max(s.reshape(CK // 8, 8, QB), axis=0))

    empty = jnp.full((8, QB), -3e38, jnp.float32)

    def step(block, head, top, next_block):
        queries = load_queries(next_block, 1 - head)
        next_top = empty
        total = jnp.zeros((8, QB), jnp.float32)
        mixed = jnp.zeros((64, QB), jnp.float32)
        row_top = jnp.max(top, axis=0, keepdims=True)
        for chunk in range(NK // CK):
            next_top = score_chunk(chunk, queries, 1 - head, next_top)
            rows = slice(chunk * CK, (chunk + 1) * CK)
            weights = jnp.exp2((scores[head][rows, :] - row_top) * SCALE)
            total = total + jnp.sum(weights.reshape(CK // 8, 8, QB), axis=0)
            mixed = mixed + matmul(
                values_t[64 * head : 64 * head + 64, rows], weights.astype(jnp.bfloat16), ((1,), (0,))
            )
        return next_top, mixed / jnp.sum(total, axis=0, keepdims=True)

    top = empty
    queries = load_queries(0, 0)
    for chunk in range(NK // CK):
        top = score_chunk(chunk, queries, 0, top)

    blocks = NQ // QB
    query = lax.broadcasted_iota(jnp.int32, (1, QB), 1)

    def body(block, top):
        top, first = step(block, 0, top, block)
        top, second = step(block, 1, top, jnp.minimum(block + 1, blocks - 1))
        chip = 2 * block + query // TILE
        live = (2 * chip + core) * TILE + query % TILE < length
        both = jnp.where(live, jnp.concatenate([first, second], axis=0), 0.0).T.astype(jnp.bfloat16)
        o_ref[2 * block] = both[:TILE]
        o_ref[2 * block + 1] = both[TILE:]
        return top

    lax.fori_loop(0, blocks, body, top)


def attention(core, length, own, sibling, masks):
    def tokens(which):
        return pl.BlockSpec((CHIPS, 1, TILE, PAIR), lambda pair: (0, which, 0, pair))

    return pl.pallas_call(
        attend,
        grid=(PAIRS,),
        out_shape=jax.ShapeDtypeStruct((CHIPS, TILE, PAIRS * PAIR), jnp.bfloat16),
        in_specs=[
            pl.BlockSpec(memory_space=pltpu.SMEM),
            pl.BlockSpec(memory_space=pltpu.SMEM),
            tokens(0), tokens(1), tokens(2), tokens(1), tokens(2),
            pl.BlockSpec((2, 16, PAIR), lambda pair: (pair, 0, 0)),
        ],
        out_specs=pl.BlockSpec((CHIPS, TILE, PAIR), lambda pair: (0, 0, pair)),
        scratch_shapes=[
            pltpu.VMEM((NK, PAIR), jnp.bfloat16),
            pltpu.VMEM((2, NK, PAIR), jnp.bfloat16),
            pltpu.VMEM((PAIR, NK), jnp.bfloat16),
            pltpu.VMEM((NK, QB), jnp.float32),
            pltpu.VMEM((NK, QB), jnp.float32),
        ],
        compiler_params=pltpu.CompilerParams(vmem_limit_bytes=40 * 2**20),
        cost_estimate=pl.CostEstimate(
            flops=4 * 6 * NQ * NK * 64, bytes_accessed=8 * 2**20, transcendentals=6 * NQ * NK
        ),
    )(core, length, own, own, own, sibling, sibling, masks)


def split_kernel(q_ref, k_ref, v_ref, packed_ref):
    packed_ref[0, 0] = q_ref[0]
    packed_ref[0, 1] = k_ref[0]
    packed_ref[0, 2] = v_ref[0]


def split_columns(*arrays):
    columns = pl.BlockSpec((1, TILE, PAIRS * PAIR), lambda chip: (0, 0, chip))
    return pl.pallas_call(
        split_kernel,
        grid=(CHIPS,),
        out_shape=jax.ShapeDtypeStruct((CHIPS, 3, TILE, PAIRS * PAIR), jnp.bfloat16),
        in_specs=[columns] * 3,
        out_specs=pl.BlockSpec((1, 3, TILE, PAIRS * PAIR), lambda chip: (chip, 0, 0, 0)),
    )(*arrays)


def join_kernel(block_ref, rows_ref):
    rows_ref[...] = block_ref[...]


def join_columns(blocks):
    return pl.pallas_call(
        join_kernel,
        grid=(CHIPS,),
        out_shape=jax.ShapeDtypeStruct((1, TILE, CHIPS * PAIRS * PAIR), jnp.bfloat16),
        in_specs=[pl.BlockSpec((1, TILE, PAIRS * PAIR), lambda chip: (chip, 0, 0))],
        out_specs=pl.BlockSpec((1, TILE, PAIRS * PAIR), lambda chip: (0, 0, chip)),
    )(blocks)


def on_device(queries, key_states, value_states, clip_lengths, tile_masks):
    place = lax.axis_index("seq")
    core = place % 2
    length = lax.dynamic_slice_in_dim(clip_lengths, lax.axis_index("clip"), 1, 0)

    mine = jnp.pad(tile_masks[0], ((0, 0), (0, 0), (0, 48)))
    mine = jnp.concatenate([mine, mine], axis=-1)
    other = lax.ppermute(mine, "seq", OTHER_CORE)
    masks = jnp.where(core == 0, jnp.concatenate([mine, other]), jnp.concatenate([other, mine]))

    packed = split_columns(queries, key_states, value_states)
    own = lax.all_to_all(packed, "seq", 0, 0, tiled=True, axis_index_groups=ALL_CHIPS)
    sibling = lax.ppermute(own, "seq", OTHER_CORE)
    mixed = attention(core.reshape(1), length, own, sibling, masks)
    back = lax.all_to_all(mixed, "seq", 0, 0, tiled=True, axis_index_groups=ALL_CHIPS)
    return join_columns(back)


def solution(mesh):
    split = P("clip", "seq", None)
    return jax.shard_map(
        on_device,
        mesh=mesh,
        in_specs=(split, split, split, P(), P("clip", "seq", None, None)),
        out_specs=split,
        check_vma=False,
    )
```

```python
import functools

import jax
import jax.numpy as jnp
from jax import lax
from jax.experimental import pallas as pl
from jax.experimental.pallas import tpu as pltpu
from jax.sharding import PartitionSpec as P

TILE = 128
CHIPS = 8
PAIR = 128
PAIRS = 3
WIDTH = PAIRS * PAIR
QB = 2 * TILE
KB = 4 * TILE
CK = 256
MASKED = -1e30
SCALE = 0.125 * 1.4426950408889634

AWAY = ((0, 0), (1, 0), (1, 1), (3, 0), (3, 1), (2, 1), (0, 1), (2, 0))
WAVES = ((0, 1, 2), (3,))
OTHER_CORE = [(device, device ^ 1) for device in range(2 * CHIPS)]


def route(along_y, along_z):
    pairs = []
    for device in range(2 * CHIPS):
        y, z, core = device // 4, device // 2 % 2, device % 2
        pairs.append((device, (y + along_y) % 4 * 4 + (z ^ along_z) * 2 + core))
    return pairs


def matmul(a, b, dims):
    return lax.dot_general(a, b, (dims, ((), ())), preferred_element_type=jnp.float32)


def whereabouts():
    device = lax.axis_index("seq").astype(jnp.int32)
    y, z, core = device // 4, device // 2 % 2, device % 2
    to_chips = [(y + along_y) % 4 * 2 + (z + along_z) % 2 for along_y, along_z in AWAY]
    from_chips = [(y + 4 - along_y) % 4 * 2 + (z + along_z) % 2 for along_y, along_z in AWAY]
    return core, to_chips, from_chips


def wave_kernel(wave, lengths_ref, *refs):
    last = wave == len(WAVES) - 1
    new = WAVES[wave]
    seen = new[0]
    if wave == 0:
        mask_ref, other_mask_ref, *refs = refs
    else:
        bias_ref, *refs = refs
    blocks, others, refs = refs[: 2 * len(new)], refs[2 * len(new) : 3 * len(new)], refs[3 * len(new) :]
    old = [refs[i * 5 : i * 5 + 5] for i in range(seen)]
    refs = refs[5 * seen :]
    if last:
        out_ref, *refs = refs
    if wave == 0:
        bias_ref, *refs = refs
    made = [refs[3 * i : 3 * i + 3] for i in range(len(new))]
    refs = refs[3 * len(new) :]
    if not last:
        new_state = [refs[2 * u : 2 * u + 2] for u in range(seen + len(new))]
        refs = refs[2 * (seen + len(new)) :]
    scores = refs

    core, _, chips = whereabouts()
    length = lengths_ref[lax.axis_index("clip")]
    low = lax.broadcasted_iota(jnp.int32, (1, PAIR), 1) < 64
    column = lax.broadcasted_iota(jnp.int32, (TILE, PAIR), 1) & 63
    inside = lax.broadcasted_iota(jnp.int32, (TILE, PAIR), 0)

    if wave == 0:
        spread = (column[:16] == inside[:16]).astype(jnp.float32).astype(jnp.bfloat16)
        for number in range(2 * PAIRS):
            local = number % 3
            kept = jnp.where(core == number // 3, mask_ref[0, local], other_mask_ref[0, local])
            kept = matmul((kept - 1).astype(jnp.float32).astype(jnp.bfloat16), spread, ((1,), (0,)))
            bias_ref[number] = jnp.where(column[:16] == 16, MASKED, kept * -MASKED)

    for slot, block in enumerate(blocks):
        keys_new, values_new, queries_new = made[slot // 2]
        chip = chips[2 * seen + slot]
        for part in range(2):
            first = (2 * part + slot % 2) * TILE
            rows = slice(first, first + TILE)
            tile = 2 * chip + (core if part == 0 else 1 - core)
            dead = jnp.where(tile * TILE + inside >= length, 16, -1)
            hot = (column == tile) | (column == dead)
            hot = hot.astype(jnp.float32).astype(jnp.bfloat16)
            for pair in range(PAIRS):
                columns = slice(pair * PAIR, (pair + 1) * PAIR)
                if part == 0:
                    k, v = block[1, :, columns], block[2, :, columns]
                else:
                    other = others[slot // 2]
                    k, v = other[slot % 2, 0, :, columns], other[slot % 2, 1, :, columns]
                keys_new[2 * pair, rows, :] = jnp.where(low, k, hot)
                keys_new[2 * pair + 1, rows, :] = jnp.where(low, hot, k)
                values_new[columns, rows] = v.T
        first = slot % 2 * TILE
        for number in range(2 * PAIRS):
            bias = bias_ref[number, pl.ds(2 * chip + core, 1), :]
            bias = jnp.broadcast_to(bias, (TILE, PAIR)).astype(jnp.bfloat16)
            q = block[0, :, number // 2 * PAIR : (number // 2 + 1) * PAIR]
            q = jnp.where(low, q, bias) if number % 2 == 0 else jnp.where(low, bias, q)
            queries_new[number, first : first + TILE, :] = q

    keys = [group[0] for group in old + made]
    values = [group[1] for group in old + made]
    queries = [group[2] for group in old + made]

    every = tuple(range(seen + len(new)))
    items = []
    if seen:
        items += [(head, [(u, new) for u in range(seen)]) for head in range(2)]
    items += [(head, [(u, every)]) for u in new for head in range(2)]

    def chunks(item):
        return [(u, group, part) for u, groups in item[1] for group in groups for part in range(KB // CK)]

    def score_chunk(pair, index, place, tops):
        head = items[index][0]
        u, group, part = chunks(items[index])[place]
        number = 2 * pair + head
        s = matmul(keys[group][number, part * CK : (part + 1) * CK, :], queries[u][number], ((1,), (1,)))
        scores[index % 2][place * CK : (place + 1) * CK, :] = s
        top = jnp.max(s.reshape(CK // 8, 8, QB), axis=0)
        return {**tops, u: jnp.maximum(tops[u], top) if u in tops else top}

    def one_pair(pair, tops):
        finished = {}
        columns = pl.ds(pl.multiple_of(pair * PAIR, PAIR), PAIR)
        for index, item in enumerate(items):
            head = item[0]
            dims = pl.ds(pl.multiple_of(pair * PAIR + 64 * head, 64), 64)
            row_top, total, mixed = {}, {}, {}
            for u, _ in item[1]:
                row_top[u] = jnp.max(tops[u], axis=0, keepdims=True)
                total[u] = jnp.zeros((8, QB), jnp.float32)
                mixed[u] = jnp.zeros((64, QB), jnp.float32)
                if u < seen:
                    before = old[u][3][pair, head : head + 1, :]
                    row_top[u] = jnp.maximum(row_top[u], before)
                    fade = jnp.exp2((before - row_top[u]) * SCALE)
                    mixed[u] = old[u][4][dims, :] * fade
                    faded = old[u][3][pair, 8 + head : 9 + head, :] * fade
                    total[u] = jnp.where(lax.broadcasted_iota(jnp.int32, (8, QB), 0) == 0, faded, 0.0)
            now = chunks(item)
            following = (index + 1) % len(items)
            next_pair = pair if following else jnp.minimum(pair + 1, PAIRS - 1)
            later = len(chunks(items[following]))
            tops = {}
            done = 0
            for place, (u, group, part) in enumerate(now):
                until = (place + 1) * later // len(now)
                while done < until:
                    tops = score_chunk(next_pair, following, done, tops)
                    done += 1
                s = scores[index % 2][place * CK : (place + 1) * CK, :]
                weights = jnp.exp2((s - row_top[u]) * SCALE)
                total[u] = total[u] + jnp.sum(weights.reshape(CK // 8, 8, QB), axis=0)
                mixed[u] = mixed[u] + matmul(
                    values[group][dims, part * CK : (part + 1) * CK], weights.astype(jnp.bfloat16), ((1,), (0,))
                )
            for u, _ in item[1]:
                total[u] = jnp.sum(total[u], axis=0, keepdims=True)
                if not last:
                    new_state[u][0][pair, head : head + 1, :] = row_top[u]
                    new_state[u][0][pair, 8 + head : 9 + head, :] = total[u]
                    new_state[u][1][dims, :] = mixed[u]
                    continue
                finished[u, head] = mixed[u] / total[u]
                if head == 1:
                    query = lax.broadcasted_iota(jnp.int32, (1, QB), 1)
                    two = chips[2 * u : 2 * u + 2]
                    chip = jnp.where(query < TILE, two[0], two[1])
                    live = (2 * chip + core) * TILE + (query & (TILE - 1)) < length
                    both = jnp.concatenate([finished[u, 0], finished[u, 1]], axis=0)
                    both = jnp.where(live, both, 0.0).T.astype(jnp.bfloat16)
                    out_ref[two[0], :, columns] = both[:TILE]
                    out_ref[two[1], :, columns] = both[TILE:]
        return tops

    tops = {}
    for place in range(len(chunks(items[0]))):
        tops = score_chunk(0, 0, place, tops)
    lax.fori_loop(0, PAIRS, one_pair, tops)


def attend_wave(wave, lengths, masks, blocks, others, old):
    last = wave == len(WAVES) - 1
    new = WAVES[wave]
    bf16, f32 = jnp.bfloat16, jnp.float32
    kept = [((2 * PAIRS, KB, PAIR), bf16), ((WIDTH, KB), bf16), ((2 * PAIRS, QB, PAIR), bf16)] * len(new)
    groups = new[0] + len(new)
    made = [((2 * PAIRS, 16, PAIR), f32)] if wave == 0 else []
    made += kept + [((PAIRS, 16, QB), f32), ((WIDTH, QB), f32)] * groups
    operands = (lengths, *masks, *blocks, *others, *[array for group in old for array in group])
    scratch = [pltpu.VMEM((groups * KB, QB), f32)] * 2
    if last:
        out_shape = jax.ShapeDtypeStruct((CHIPS, TILE, WIDTH), bf16)
        scratch = [pltpu.VMEM(*array) for array in made[: len(made) - 2 * groups]] + scratch
        out_specs = pl.BlockSpec(memory_space=pltpu.VMEM)
    else:
        out_shape = [jax.ShapeDtypeStruct(*array) for array in made]
        out_specs = [pl.BlockSpec(memory_space=pltpu.VMEM)] * len(out_shape)
    out = pl.pallas_call(
        functools.partial(wave_kernel, wave),
        out_shape=out_shape,
        in_specs=[pl.BlockSpec(memory_space=pltpu.SMEM)]
        + [pl.BlockSpec(memory_space=pltpu.VMEM)] * (len(operands) - 1),
        out_specs=out_specs,
        scratch_shapes=scratch,
        compiler_params=pltpu.CompilerParams(vmem_limit_bytes=32 * 2**20),
        cost_estimate=pl.CostEstimate(flops=0, bytes_accessed=0, transcendentals=0),
    )(*operands)
    if last:
        return out
    if wave == 0:
        masks, out = out[:1], out[1:]
    kept, states = out[: 3 * len(new)], out[3 * len(new) :]
    parts = [group[:3] for group in old] + [kept[3 * i : 3 * i + 3] for i in range(len(new))]
    return masks, [(*part, *states[2 * u : 2 * u + 2]) for u, part in enumerate(parts)]


def split_kernel(q_ref, k_ref, v_ref, *refs):
    _, chips, _ = whereabouts()
    blocks, done = refs[:-1], refs[-1]
    copies = []
    for chip, block in zip(chips, blocks):
        columns = pl.ds(pl.multiple_of(chip * WIDTH, PAIR), WIDTH)
        for which, array in enumerate((q_ref, k_ref, v_ref)):
            copies.append(pltpu.make_async_copy(array.at[0, :, columns], block.at[which], done.at[len(copies)]))
    for copy in copies:
        copy.start()
    for copy in copies:
        copy.wait()


def split_columns(*arrays):
    return pl.pallas_call(
        split_kernel,
        out_shape=[jax.ShapeDtypeStruct((3, TILE, WIDTH), jnp.bfloat16)] * CHIPS,
        in_specs=[pl.BlockSpec(memory_space=pl.ANY)] * 3,
        out_specs=[pl.BlockSpec(memory_space=pltpu.VMEM)] * CHIPS,
        scratch_shapes=[pltpu.SemaphoreType.DMA((3 * CHIPS,))],
    )(*arrays)


def join_kernel(blocks_ref, rows_ref, done):
    copies = [
        pltpu.make_async_copy(
            blocks_ref.at[chip], rows_ref.at[0, :, pl.ds(chip * WIDTH, WIDTH)], done.at[chip]
        )
        for chip in range(CHIPS)
    ]
    for copy in copies:
        copy.start()
    for copy in copies:
        copy.wait()


def join_columns(blocks):
    return pl.pallas_call(
        join_kernel,
        out_shape=jax.ShapeDtypeStruct((1, TILE, CHIPS * WIDTH), jnp.bfloat16),
        in_specs=[pl.BlockSpec(memory_space=pltpu.VMEM)],
        out_specs=pl.BlockSpec(memory_space=pl.ANY),
        scratch_shapes=[pltpu.SemaphoreType.DMA((CHIPS,))],
    )(blocks)


def after(array, earlier):
    return lax.optimization_barrier((array, earlier))[0]


def on_device(queries, key_states, value_states, clip_lengths, tile_masks):
    masks = tile_masks, lax.ppermute(tile_masks, "seq", OTHER_CORE)
    sent = list(split_columns(queries, key_states, value_states))
    sent[3] = after(sent[3], masks[1])
    blocks = [sent[0]]
    for slot in range(1, CHIPS):
        blocks.append(lax.ppermute(sent[slot], "seq", route(*AWAY[slot])))

    groups = []
    for wave, new in enumerate(WAVES):
        now = blocks[2 * new[0] : 2 * new[-1] + 2]
        if wave > 0:
            now = after(now, groups[0][3])
        others = [
            lax.ppermute(jnp.stack([block[1:] for block in now[i : i + 2]]), "seq", OTHER_CORE)
            for i in range(0, len(now), 2)
        ]
        out = attend_wave(wave, clip_lengths, masks, now, others, groups)
        if wave < len(WAVES) - 1:
            masks, groups = out

    every = [[2 * chip + core for chip in range(CHIPS)] for core in range(2)]
    back = lax.all_to_all(out, "seq", 0, 0, tiled=True, axis_index_groups=every)
    return join_columns(back)


def solution(mesh):
    split = P("clip", "seq", None)
    return jax.shard_map(
        on_device,
        mesh=mesh,
        in_specs=(split, split, split, P(), P("clip", "seq", None, None)),
        out_specs=split,
        check_vma=False,
    )
```

```python
import functools

import jax
import jax.numpy as jnp
from jax import lax
from jax.experimental import pallas as pl
from jax.experimental.pallas import tpu as pltpu
from jax.sharding import PartitionSpec as P

TILE = 128
CHIPS = 8
PAIR = 128
PAIRS = 3
WIDTH = PAIRS * PAIR
QB = 2 * TILE
KB = 4 * TILE
CK = 256
MASKED = -1e30
SCALE = 0.125 * 1.4426950408889634

AWAY = ((0, 0), (1, 0), (1, 1), (3, 0), (3, 1), (2, 1), (0, 1), (2, 0))
WAVES = ((0, 1, 2), (3,))
SPLITS = ((5,), (1, 2, 3, 4), (0, 6, 7))
OTHER_CORE = [(device, device ^ 1) for device in range(2 * CHIPS)]


def route(along_y, along_z):
    pairs = []
    for device in range(2 * CHIPS):
        y, z, core = device // 4, device // 2 % 2, device % 2
        pairs.append((device, (y + along_y) % 4 * 4 + (z ^ along_z) * 2 + core))
    return pairs


def matmul(a, b, dims):
    return lax.dot_general(a, b, (dims, ((), ())), preferred_element_type=jnp.float32)


def whereabouts():
    device = lax.axis_index("seq").astype(jnp.int32)
    y, z, core = device // 4, device // 2 % 2, device % 2
    to_chips = [(y + along_y) % 4 * 2 + (z + along_z) % 2 for along_y, along_z in AWAY]
    from_chips = [(y + 4 - along_y) % 4 * 2 + (z + along_z) % 2 for along_y, along_z in AWAY]
    return core, to_chips, from_chips


def wave_kernel(wave, lengths_ref, *refs):
    last = wave == len(WAVES) - 1
    new = WAVES[wave]
    seen = new[0]
    if wave == 0:
        mask_ref, other_mask_ref, *refs = refs
    else:
        bias_ref, *refs = refs
    blocks, others, refs = refs[: 2 * len(new)], refs[2 * len(new) : 3 * len(new)], refs[3 * len(new) :]
    old = [refs[i * 5 : i * 5 + 5] for i in range(seen)]
    refs = refs[5 * seen :]
    if last:
        out_ref, *refs = refs
    if wave == 0:
        bias_ref, *refs = refs
    made = [refs[3 * i : 3 * i + 3] for i in range(len(new))]
    refs = refs[3 * len(new) :]
    if not last:
        new_state = [refs[2 * u : 2 * u + 2] for u in range(seen + len(new))]
        refs = refs[2 * (seen + len(new)) :]
    scores = refs

    core, _, chips = whereabouts()
    length = lengths_ref[lax.axis_index("clip")]
    low = lax.broadcasted_iota(jnp.int32, (1, PAIR), 1) < 64
    column = lax.broadcasted_iota(jnp.int32, (TILE, PAIR), 1) & 63
    inside = lax.broadcasted_iota(jnp.int32, (TILE, PAIR), 0)

    if wave == 0:
        spread = (column[:16] == inside[:16]).astype(jnp.float32).astype(jnp.bfloat16)
        for number in range(2 * PAIRS):
            local = number % 3
            kept = jnp.where(core == number // 3, mask_ref[0, local], other_mask_ref[0, local])
            kept = matmul((kept - 1).astype(jnp.float32).astype(jnp.bfloat16), spread, ((1,), (0,)))
            bias_ref[number] = jnp.where(column[:16] == 16, MASKED, kept * -MASKED)

    for slot, block in enumerate(blocks):
        keys_new, values_new, queries_new = made[slot // 2]
        chip = chips[2 * seen + slot]
        for part in range(2):
            first = (2 * part + slot % 2) * TILE
            rows = slice(first, first + TILE)
            tile = 2 * chip + (core if part == 0 else 1 - core)
            dead = jnp.where(tile * TILE + inside >= length, 16, -1)
            hot = (column == tile) | (column == dead)
            hot = hot.astype(jnp.float32).astype(jnp.bfloat16)
            for pair in range(PAIRS):
                columns = slice(pair * PAIR, (pair + 1) * PAIR)
                if part == 0:
                    k, v = block[1, :, columns], block[2, :, columns]
                else:
                    other = others[slot // 2]
                    k, v = other[slot % 2, 0, :, columns], other[slot % 2, 1, :, columns]
                keys_new[2 * pair, rows, :] = jnp.where(low, k, hot)
                keys_new[2 * pair + 1, rows, :] = jnp.where(low, hot, k)
                values_new[columns, rows] = v.T
        first = slot % 2 * TILE
        for number in range(2 * PAIRS):
            bias = bias_ref[number, pl.ds(2 * chip + core, 1), :]
            bias = jnp.broadcast_to(bias, (TILE, PAIR)).astype(jnp.bfloat16)
            q = block[0, :, number // 2 * PAIR : (number // 2 + 1) * PAIR]
            q = jnp.where(low, q, bias) if number % 2 == 0 else jnp.where(low, bias, q)
            queries_new[number, first : first + TILE, :] = q

    keys = [group[0] for group in old + made]
    values = [group[1] for group in old + made]
    queries = [group[2] for group in old + made]

    every = tuple(range(seen + len(new)))
    items = []
    if seen:
        items += [(head, [(u, new) for u in range(seen)]) for head in range(2)]
    items += [(head, [(u, every)]) for u in new for head in range(2)]

    def chunks(item):
        return [(u, group, part) for u, groups in item[1] for group in groups for part in range(KB // CK)]

    def score_chunk(pair, index, place, tops):
        head = items[index][0]
        u, group, part = chunks(items[index])[place]
        number = 2 * pair + head
        s = matmul(keys[group][number, part * CK : (part + 1) * CK, :], queries[u][number], ((1,), (1,)))
        scores[index % 2][place * CK : (place + 1) * CK, :] = s
        top = jnp.max(s.reshape(CK // 8, 8, QB), axis=0)
        return {**tops, u: jnp.maximum(tops[u], top) if u in tops else top}

    def one_pair(pair, tops):
        finished = {}
        columns = pl.ds(pl.multiple_of(pair * PAIR, PAIR), PAIR)
        for index, item in enumerate(items):
            head = item[0]
            dims = pl.ds(pl.multiple_of(pair * PAIR + 64 * head, 64), 64)
            row_top, total, mixed = {}, {}, {}
            for u, _ in item[1]:
                row_top[u] = jnp.max(tops[u], axis=0, keepdims=True)
                total[u] = jnp.zeros((8, QB), jnp.float32)
                mixed[u] = jnp.zeros((64, QB), jnp.float32)
                if u < seen:
                    before = old[u][3][pair, head : head + 1, :]
                    row_top[u] = jnp.maximum(row_top[u], before)
                    fade = jnp.exp2((before - row_top[u]) * SCALE)
                    mixed[u] = old[u][4][dims, :] * fade
                    faded = old[u][3][pair, 8 + head : 9 + head, :] * fade
                    total[u] = jnp.where(lax.broadcasted_iota(jnp.int32, (8, QB), 0) == 0, faded, 0.0)
            now = chunks(item)
            following = (index + 1) % len(items)
            next_pair = pair if following else jnp.minimum(pair + 1, PAIRS - 1)
            later = len(chunks(items[following]))
            tops = {}
            done = 0
            for place, (u, group, part) in enumerate(now):
                until = (place + 1) * later // len(now)
                while done < until:
                    tops = score_chunk(next_pair, following, done, tops)
                    done += 1
                s = scores[index % 2][place * CK : (place + 1) * CK, :]
                weights = jnp.exp2((s - row_top[u]) * SCALE)
                total[u] = total[u] + jnp.sum(weights.reshape(CK // 8, 8, QB), axis=0)
                mixed[u] = mixed[u] + matmul(
                    values[group][dims, part * CK : (part + 1) * CK], weights.astype(jnp.bfloat16), ((1,), (0,))
                )
            for u, _ in item[1]:
                total[u] = jnp.sum(total[u], axis=0, keepdims=True)
                if not last:
                    new_state[u][0][pair, head : head + 1, :] = row_top[u]
                    new_state[u][0][pair, 8 + head : 9 + head, :] = total[u]
                    new_state[u][1][dims, :] = mixed[u]
                    continue
                finished[u, head] = mixed[u] / total[u]
                if head == 1:
                    query = lax.broadcasted_iota(jnp.int32, (1, QB), 1)
                    two = chips[2 * u : 2 * u + 2]
                    chip = jnp.where(query < TILE, two[0], two[1])
                    live = (2 * chip + core) * TILE + (query & (TILE - 1)) < length
                    both = jnp.concatenate([finished[u, 0], finished[u, 1]], axis=0)
                    both = jnp.where(live, both, 0.0).T.astype(jnp.bfloat16)
                    out_ref[two[0], :, columns] = both[:TILE]
                    out_ref[two[1], :, columns] = both[TILE:]
        return tops

    tops = {}
    for place in range(len(chunks(items[0]))):
        tops = score_chunk(0, 0, place, tops)
    lax.fori_loop(0, PAIRS, one_pair, tops)


def attend_wave(wave, lengths, masks, blocks, others, old):
    last = wave == len(WAVES) - 1
    new = WAVES[wave]
    bf16, f32 = jnp.bfloat16, jnp.float32
    kept = [((2 * PAIRS, KB, PAIR), bf16), ((WIDTH, KB), bf16), ((2 * PAIRS, QB, PAIR), bf16)] * len(new)
    groups = new[0] + len(new)
    made = [((2 * PAIRS, 16, PAIR), f32)] if wave == 0 else []
    made += kept + [((PAIRS, 16, QB), f32), ((WIDTH, QB), f32)] * groups
    operands = (lengths, *masks, *blocks, *others, *[array for group in old for array in group])
    scratch = [pltpu.VMEM((groups * KB, QB), f32)] * 2
    if last:
        out_shape = jax.ShapeDtypeStruct((CHIPS, TILE, WIDTH), bf16)
        scratch = [pltpu.VMEM(*array) for array in made[: len(made) - 2 * groups]] + scratch
        out_specs = pl.BlockSpec(memory_space=pltpu.VMEM)
    else:
        out_shape = [jax.ShapeDtypeStruct(*array) for array in made]
        out_specs = [pl.BlockSpec(memory_space=pltpu.VMEM)] * len(out_shape)
    out = pl.pallas_call(
        functools.partial(wave_kernel, wave),
        out_shape=out_shape,
        in_specs=[pl.BlockSpec(memory_space=pltpu.SMEM)]
        + [pl.BlockSpec(memory_space=pltpu.VMEM)] * (len(operands) - 1),
        out_specs=out_specs,
        scratch_shapes=scratch,
        compiler_params=pltpu.CompilerParams(vmem_limit_bytes=32 * 2**20),
        cost_estimate=pl.CostEstimate(flops=0, bytes_accessed=0, transcendentals=0),
    )(*operands)
    if last:
        return out
    if wave == 0:
        masks, out = out[:1], out[1:]
    kept, states = out[: 3 * len(new)], out[3 * len(new) :]
    parts = [group[:3] for group in old] + [kept[3 * i : 3 * i + 3] for i in range(len(new))]
    return masks, [(*part, *states[2 * u : 2 * u + 2]) for u, part in enumerate(parts)]


def split_kernel(slots, q_ref, k_ref, v_ref, *refs):
    _, chips, _ = whereabouts()
    blocks, done = refs[:-1], refs[-1]
    copies = []
    for slot, block in zip(slots, blocks):
        columns = pl.ds(pl.multiple_of(chips[slot] * WIDTH, PAIR), WIDTH)
        for which, array in enumerate((q_ref, k_ref, v_ref)):
            copies.append(pltpu.make_async_copy(array.at[0, :, columns], block.at[which], done.at[len(copies)]))
    for copy in copies:
        copy.start()
    for copy in copies:
        copy.wait()


def split_columns(slots, *arrays):
    return pl.pallas_call(
        functools.partial(split_kernel, slots),
        out_shape=[jax.ShapeDtypeStruct((3, TILE, WIDTH), jnp.bfloat16)] * len(slots),
        in_specs=[pl.BlockSpec(memory_space=pl.ANY)] * 3,
        out_specs=[pl.BlockSpec(memory_space=pltpu.VMEM)] * len(slots),
        scratch_shapes=[pltpu.SemaphoreType.DMA((3 * len(slots),))],
    )(*arrays)


def join_kernel(blocks_ref, rows_ref, done):
    copies = [
        pltpu.make_async_copy(
            blocks_ref.at[chip], rows_ref.at[0, :, pl.ds(chip * WIDTH, WIDTH)], done.at[chip]
        )
        for chip in range(CHIPS)
    ]
    for copy in copies:
        copy.start()
    for copy in copies:
        copy.wait()


def join_columns(blocks):
    return pl.pallas_call(
        join_kernel,
        out_shape=jax.ShapeDtypeStruct((1, TILE, CHIPS * WIDTH), jnp.bfloat16),
        in_specs=[pl.BlockSpec(memory_space=pltpu.VMEM)],
        out_specs=pl.BlockSpec(memory_space=pl.ANY),
        scratch_shapes=[pltpu.SemaphoreType.DMA((CHIPS,))],
    )(blocks)


def after(array, earlier):
    return lax.optimization_barrier((array, earlier))[0]


def on_device(queries, key_states, value_states, clip_lengths, tile_masks):
    masks = tile_masks, lax.ppermute(tile_masks, "seq", OTHER_CORE)
    sent = [None] * CHIPS
    for slots in SPLITS:
        for slot, block in zip(slots, split_columns(slots, queries, key_states, value_states)):
            sent[slot] = block
    blocks = [sent[0]]
    for slot in range(1, CHIPS):
        blocks.append(lax.ppermute(sent[slot], "seq", route(*AWAY[slot])))

    groups = []
    for wave, new in enumerate(WAVES):
        now = blocks[2 * new[0] : 2 * new[-1] + 2]
        if wave > 0:
            now = after(now, groups[0][3])
        others = [
            lax.ppermute(jnp.stack([block[1:] for block in now[i : i + 2]]), "seq", OTHER_CORE)
            for i in range(0, len(now), 2)
        ]
        out = attend_wave(wave, clip_lengths, masks, now, others, groups)
        if wave < len(WAVES) - 1:
            masks, groups = out

    every = [[2 * chip + core for chip in range(CHIPS)] for core in range(2)]
    back = lax.all_to_all(out, "seq", 0, 0, tiled=True, axis_index_groups=every)
    return join_columns(back)


def solution(mesh):
    split = P("clip", "seq", None)
    return jax.shard_map(
        on_device,
        mesh=mesh,
        in_specs=(split, split, split, P(), P("clip", "seq", None, None)),
        out_specs=split,
        check_vma=False,
    )
```

```python
import functools

import jax
import jax.numpy as jnp
from jax import lax
from jax.experimental import pallas as pl
from jax.experimental.pallas import tpu as pltpu
from jax.sharding import PartitionSpec as P

TILE = 128
CHIPS = 8
PAIR = 128
PAIRS = 3
WIDTH = PAIRS * PAIR
QB = 2 * TILE
KB = 4 * TILE
CK = 256
MASKED = -1e30
SCALE = 0.125 * 1.4426950408889634

AWAY = ((0, 0), (1, 0), (1, 1), (3, 0), (3, 1), (2, 1), (0, 1), (2, 0))
WAVES = ((0, 1, 2), (3,))
SPLITS = ((5,), (1, 2, 3, 4), (0, 6, 7))
OTHER_CORE = [(device, device ^ 1) for device in range(2 * CHIPS)]


def route(along_y, along_z):
    pairs = []
    for device in range(2 * CHIPS):
        y, z, core = device // 4, device // 2 % 2, device % 2
        pairs.append((device, (y + along_y) % 4 * 4 + (z ^ along_z) * 2 + core))
    return pairs


def matmul(a, b, dims):
    return lax.dot_general(a, b, (dims, ((), ())), preferred_element_type=jnp.float32)


def whereabouts():
    device = lax.axis_index("seq").astype(jnp.int32)
    y, z, core = device // 4, device // 2 % 2, device % 2
    to_chips = [(y + along_y) % 4 * 2 + (z + along_z) % 2 for along_y, along_z in AWAY]
    from_chips = [(y + 4 - along_y) % 4 * 2 + (z + along_z) % 2 for along_y, along_z in AWAY]
    return core, to_chips, from_chips


def wave_kernel(wave, lengths_ref, *refs):
    last = wave == len(WAVES) - 1
    new = WAVES[wave]
    seen = new[0]
    if wave == 0:
        mask_ref, other_mask_ref, *refs = refs
    else:
        bias_ref, *refs = refs
    blocks, others, refs = refs[: 2 * len(new)], refs[2 * len(new) : 3 * len(new)], refs[3 * len(new) :]
    old = [refs[i * 5 : i * 5 + 5] for i in range(seen)]
    refs = refs[5 * seen :]
    if last:
        out_ref, *refs = refs
    if wave == 0:
        bias_ref, *refs = refs
    made = [refs[3 * i : 3 * i + 3] for i in range(len(new))]
    refs = refs[3 * len(new) :]
    if not last:
        new_state = [refs[2 * u : 2 * u + 2] for u in range(seen + len(new))]
        refs = refs[2 * (seen + len(new)) :]
    scores = refs

    core, _, chips = whereabouts()
    length = lengths_ref[lax.axis_index("clip")]
    low = lax.broadcasted_iota(jnp.int32, (1, PAIR), 1) < 64
    column = lax.broadcasted_iota(jnp.int32, (TILE, PAIR), 1) & 63
    inside = lax.broadcasted_iota(jnp.int32, (TILE, PAIR), 0)

    if wave == 0:
        spread = (column[:16] == inside[:16]).astype(jnp.float32).astype(jnp.bfloat16)
        for number in range(2 * PAIRS):
            local = number % 3
            kept = jnp.where(core == number // 3, mask_ref[0, local], other_mask_ref[0, local])
            kept = matmul((kept - 1).astype(jnp.float32).astype(jnp.bfloat16), spread, ((1,), (0,)))
            bias_ref[number] = jnp.where(column[:16] == 16, MASKED, kept * -MASKED)

    for slot, block in enumerate(blocks):
        keys_new, values_new, queries_new = made[slot // 2]
        chip = chips[2 * seen + slot]
        for part in range(2):
            first = (2 * part + slot % 2) * TILE
            rows = slice(first, first + TILE)
            tile = 2 * chip + (core if part == 0 else 1 - core)
            dead = jnp.where(tile * TILE + inside >= length, 16, -1)
            hot = (column == tile) | (column == dead)
            hot = hot.astype(jnp.float32).astype(jnp.bfloat16)
            for pair in range(PAIRS):
                columns = slice(pair * PAIR, (pair + 1) * PAIR)
                if part == 0:
                    k, v = block[1, :, columns], block[2, :, columns]
                else:
                    other = others[slot // 2]
                    k, v = other[slot % 2, 0, :, columns], other[slot % 2, 1, :, columns]
                keys_new[2 * pair, rows, :] = jnp.where(low, k, hot)
                keys_new[2 * pair + 1, rows, :] = jnp.where(low, hot, k)
                values_new[columns, rows] = v.T
        first = slot % 2 * TILE
        for number in range(2 * PAIRS):
            bias = bias_ref[number, pl.ds(2 * chip + core, 1), :]
            bias = jnp.broadcast_to(bias, (TILE, PAIR)).astype(jnp.bfloat16)
            q = block[0, :, number // 2 * PAIR : (number // 2 + 1) * PAIR]
            q = jnp.where(low, q, bias) if number % 2 == 0 else jnp.where(low, bias, q)
            queries_new[number, first : first + TILE, :] = q

    keys = [group[0] for group in old + made]
    values = [group[1] for group in old + made]
    queries = [group[2] for group in old + made]

    every = tuple(range(seen + len(new)))
    items = [(head, [(u, new) for u in range(seen)] + [(u, every) for u in new]) for head in range(2)]

    def chunks(item):
        return [(u, group, part) for u, groups in item[1] for group in groups for part in range(KB // CK)]

    def score_chunk(pair, index, place, tops):
        head = items[index][0]
        u, group, part = chunks(items[index])[place]
        number = 2 * pair + head
        s = matmul(keys[group][number, part * CK : (part + 1) * CK, :], queries[u][number], ((1,), (1,)))
        scores[index % 2][place * CK : (place + 1) * CK, :] = s
        top = jnp.max(s.reshape(CK // 8, 8, QB), axis=0)
        return {**tops, u: jnp.maximum(tops[u], top) if u in tops else top}

    def one_pair(pair, tops, ends=False):
        finished = {}
        columns = pl.ds(pl.multiple_of(pair * PAIR, PAIR), PAIR)
        for index, item in enumerate(items):
            head = item[0]
            dims = pl.ds(pl.multiple_of(pair * PAIR + 64 * head, 64), 64)
            row_top, total, mixed = {}, {}, {}
            for u, _ in item[1]:
                row_top[u] = jnp.max(tops[u], axis=0, keepdims=True)
                total[u] = jnp.zeros((8, QB), jnp.float32)
                mixed[u] = jnp.zeros((64, QB), jnp.float32)
                if u < seen:
                    before = old[u][3][pair, head : head + 1, :]
                    row_top[u] = jnp.maximum(row_top[u], before)
                    fade = jnp.exp2((before - row_top[u]) * SCALE)
                    mixed[u] = old[u][4][dims, :] * fade
                    faded = old[u][3][pair, 8 + head : 9 + head, :] * fade
                    total[u] = jnp.where(lax.broadcasted_iota(jnp.int32, (8, QB), 0) == 0, faded, 0.0)
            now = chunks(item)
            following = (index + 1) % len(items)
            next_pair = pair if following else pair + 1
            later = 0 if ends and not following else len(chunks(items[following]))
            tops = {}
            done = 0
            for place, (u, group, part) in enumerate(now):
                until = (place + 1) * later // len(now)
                while done < until:
                    tops = score_chunk(next_pair, following, done, tops)
                    done += 1
                s = scores[index % 2][place * CK : (place + 1) * CK, :]
                weights = jnp.exp2((s - row_top[u]) * SCALE)
                total[u] = total[u] + jnp.sum(weights.reshape(CK // 8, 8, QB), axis=0)
                mixed[u] = mixed[u] + matmul(
                    values[group][dims, part * CK : (part + 1) * CK], weights.astype(jnp.bfloat16), ((1,), (0,))
                )
            for u, _ in item[1]:
                total[u] = jnp.sum(total[u], axis=0, keepdims=True)
                if not last:
                    new_state[u][0][pair, head : head + 1, :] = row_top[u]
                    new_state[u][0][pair, 8 + head : 9 + head, :] = total[u]
                    new_state[u][1][dims, :] = mixed[u]
                    continue
                finished[u, head] = mixed[u] / total[u]
                if head == 1:
                    query = lax.broadcasted_iota(jnp.int32, (1, QB), 1)
                    two = chips[2 * u : 2 * u + 2]
                    chip = jnp.where(query < TILE, two[0], two[1])
                    live = (2 * chip + core) * TILE + (query & (TILE - 1)) < length
                    both = jnp.concatenate([finished[u, 0], finished[u, 1]], axis=0)
                    both = jnp.where(live, both, 0.0).T.astype(jnp.bfloat16)
                    out_ref[two[0], :, columns] = both[:TILE]
                    out_ref[two[1], :, columns] = both[TILE:]
        return tops

    tops = {}
    for place in range(len(chunks(items[0]))):
        tops = score_chunk(0, 0, place, tops)
    tops = lax.fori_loop(0, PAIRS - 1, one_pair, tops)
    one_pair(PAIRS - 1, tops, ends=True)


def attend_wave(wave, lengths, masks, blocks, others, old):
    last = wave == len(WAVES) - 1
    new = WAVES[wave]
    bf16, f32 = jnp.bfloat16, jnp.float32
    kept = [((2 * PAIRS, KB, PAIR), bf16), ((WIDTH, KB), bf16), ((2 * PAIRS, QB, PAIR), bf16)] * len(new)
    groups = new[0] + len(new)
    made = [((2 * PAIRS, 16, PAIR), f32)] if wave == 0 else []
    made += kept + [((PAIRS, 16, QB), f32), ((WIDTH, QB), f32)] * groups
    operands = (lengths, *masks, *blocks, *others, *[array for group in old for array in group])
    scratch = [pltpu.VMEM(((new[0] * len(new) + len(new) * groups) * KB, QB), f32)] * 2
    if last:
        out_shape = jax.ShapeDtypeStruct((CHIPS, TILE, WIDTH), bf16)
        scratch = [pltpu.VMEM(*array) for array in made[: len(made) - 2 * groups]] + scratch
        out_specs = pl.BlockSpec(memory_space=pltpu.VMEM)
    else:
        out_shape = [jax.ShapeDtypeStruct(*array) for array in made]
        out_specs = [pl.BlockSpec(memory_space=pltpu.VMEM)] * len(out_shape)
    out = pl.pallas_call(
        functools.partial(wave_kernel, wave),
        out_shape=out_shape,
        in_specs=[pl.BlockSpec(memory_space=pltpu.SMEM)]
        + [pl.BlockSpec(memory_space=pltpu.VMEM)] * (len(operands) - 1),
        out_specs=out_specs,
        scratch_shapes=scratch,
        compiler_params=pltpu.CompilerParams(vmem_limit_bytes=32 * 2**20),
        cost_estimate=pl.CostEstimate(flops=0, bytes_accessed=0, transcendentals=0),
    )(*operands)
    if last:
        return out
    if wave == 0:
        masks, out = out[:1], out[1:]
    kept, states = out[: 3 * len(new)], out[3 * len(new) :]
    parts = [group[:3] for group in old] + [kept[3 * i : 3 * i + 3] for i in range(len(new))]
    return masks, [(*part, *states[2 * u : 2 * u + 2]) for u, part in enumerate(parts)]


def split_kernel(slots, q_ref, k_ref, v_ref, *refs):
    _, chips, _ = whereabouts()
    blocks, done = refs[:-1], refs[-1]
    copies = []
    for slot, block in zip(slots, blocks):
        columns = pl.ds(pl.multiple_of(chips[slot] * WIDTH, PAIR), WIDTH)
        for which, array in enumerate((q_ref, k_ref, v_ref)):
            copies.append(pltpu.make_async_copy(array.at[0, :, columns], block.at[which], done.at[len(copies)]))
    for copy in copies:
        copy.start()
    for copy in copies:
        copy.wait()


def split_columns(slots, *arrays):
    return pl.pallas_call(
        functools.partial(split_kernel, slots),
        out_shape=[jax.ShapeDtypeStruct((3, TILE, WIDTH), jnp.bfloat16)] * len(slots),
        in_specs=[pl.BlockSpec(memory_space=pl.ANY)] * 3,
        out_specs=[pl.BlockSpec(memory_space=pltpu.VMEM)] * len(slots),
        scratch_shapes=[pltpu.SemaphoreType.DMA((3 * len(slots),))],
    )(*arrays)


def join_kernel(blocks_ref, rows_ref, done):
    copies = [
        pltpu.make_async_copy(
            blocks_ref.at[chip], rows_ref.at[0, :, pl.ds(chip * WIDTH, WIDTH)], done.at[chip]
        )
        for chip in range(CHIPS)
    ]
    for copy in copies:
        copy.start()
    for copy in copies:
        copy.wait()


def join_columns(blocks):
    return pl.pallas_call(
        join_kernel,
        out_shape=jax.ShapeDtypeStruct((1, TILE, CHIPS * WIDTH), jnp.bfloat16),
        in_specs=[pl.BlockSpec(memory_space=pltpu.VMEM)],
        out_specs=pl.BlockSpec(memory_space=pl.ANY),
        scratch_shapes=[pltpu.SemaphoreType.DMA((CHIPS,))],
    )(blocks)


def after(array, earlier):
    return lax.optimization_barrier((array, earlier))[0]


def on_device(queries, key_states, value_states, clip_lengths, tile_masks):
    masks = tile_masks, lax.ppermute(tile_masks, "seq", OTHER_CORE)
    sent = [None] * CHIPS
    for slots in SPLITS:
        for slot, block in zip(slots, split_columns(slots, queries, key_states, value_states)):
            sent[slot] = block
    blocks = [sent[0]]
    for slot in range(1, CHIPS):
        blocks.append(lax.ppermute(sent[slot], "seq", route(*AWAY[slot])))

    groups = []
    for wave, new in enumerate(WAVES):
        now = blocks[2 * new[0] : 2 * new[-1] + 2]
        if wave > 0:
            now = after(now, groups[0][3])
        others = [
            lax.ppermute(jnp.stack([block[1:] for block in now[i : i + 2]]), "seq", OTHER_CORE)
            for i in range(0, len(now), 2)
        ]
        out = attend_wave(wave, clip_lengths, masks, now, others, groups)
        if wave < len(WAVES) - 1:
            masks, groups = out

    every = [[2 * chip + core for chip in range(CHIPS)] for core in range(2)]
    back = lax.all_to_all(out, "seq", 0, 0, tiled=True, axis_index_groups=every)
    return join_columns(back)


def solution(mesh):
    split = P("clip", "seq", None)
    return jax.shard_map(
        on_device,
        mesh=mesh,
        in_specs=(split, split, split, P(), P("clip", "seq", None, None)),
        out_specs=split,
        check_vma=False,
    )
```

```python
import functools

import jax
import jax.numpy as jnp
from jax import lax
from jax.experimental import pallas as pl
from jax.experimental.pallas import tpu as pltpu
from jax.sharding import PartitionSpec as P

TILE = 128
CHIPS = 8
PAIR = 128
PAIRS = 3
WIDTH = PAIRS * PAIR
QB = 2 * TILE
KB = 4 * TILE
CK = 512
MASKED = -1e30
SCALE = 0.125 * 1.4426950408889634

AWAY = ((0, 0), (1, 0), (1, 1), (3, 0), (3, 1), (2, 1), (0, 1), (2, 0))
WAVES = ((0, 1, 2), (3,))
SPLITS = ((5,), (1, 2, 3, 4), (0, 6, 7))
OTHER_CORE = [(device, device ^ 1) for device in range(2 * CHIPS)]


def route(along_y, along_z):
    pairs = []
    for device in range(2 * CHIPS):
        y, z, core = device // 4, device // 2 % 2, device % 2
        pairs.append((device, (y + along_y) % 4 * 4 + (z ^ along_z) * 2 + core))
    return pairs


def matmul(a, b, dims):
    return lax.dot_general(a, b, (dims, ((), ())), preferred_element_type=jnp.float32)


def whereabouts():
    device = lax.axis_index("seq").astype(jnp.int32)
    y, z, core = device // 4, device // 2 % 2, device % 2
    to_chips = [(y + along_y) % 4 * 2 + (z + along_z) % 2 for along_y, along_z in AWAY]
    from_chips = [(y + 4 - along_y) % 4 * 2 + (z + along_z) % 2 for along_y, along_z in AWAY]
    return core, to_chips, from_chips


def wave_kernel(wave, lengths_ref, *refs):
    last = wave == len(WAVES) - 1
    new = WAVES[wave]
    seen = new[0]
    if wave == 0:
        mask_ref, other_mask_ref, *refs = refs
    else:
        bias_ref, *refs = refs
    blocks, others, refs = refs[: 2 * len(new)], refs[2 * len(new) : 3 * len(new)], refs[3 * len(new) :]
    old = [refs[i * 5 : i * 5 + 5] for i in range(seen)]
    refs = refs[5 * seen :]
    if last:
        out_ref, *refs = refs
    if wave == 0:
        bias_ref, *refs = refs
    made = [refs[3 * i : 3 * i + 3] for i in range(len(new))]
    refs = refs[3 * len(new) :]
    if not last:
        new_state = [refs[2 * u : 2 * u + 2] for u in range(seen + len(new))]
        refs = refs[2 * (seen + len(new)) :]
    scores = refs

    core, _, chips = whereabouts()
    length = lengths_ref[lax.axis_index("clip")]
    low = lax.broadcasted_iota(jnp.int32, (1, PAIR), 1) < 64
    column = lax.broadcasted_iota(jnp.int32, (TILE, PAIR), 1) & 63
    inside = lax.broadcasted_iota(jnp.int32, (TILE, PAIR), 0)

    if wave == 0:
        spread = (column[:16] == inside[:16]).astype(jnp.float32).astype(jnp.bfloat16)
        for number in range(2 * PAIRS):
            local = number % 3
            kept = jnp.where(core == number // 3, mask_ref[0, local], other_mask_ref[0, local])
            kept = matmul((kept - 1).astype(jnp.float32).astype(jnp.bfloat16), spread, ((1,), (0,)))
            bias_ref[number] = jnp.where(column[:16] == 16, MASKED, kept * -MASKED)

    for slot, block in enumerate(blocks):
        keys_new, values_new, queries_new = made[slot // 2]
        chip = chips[2 * seen + slot]
        for part in range(2):
            first = (2 * part + slot % 2) * TILE
            rows = slice(first, first + TILE)
            tile = 2 * chip + (core if part == 0 else 1 - core)
            dead = jnp.where(tile * TILE + inside >= length, 16, -1)
            hot = (column == tile) | (column == dead)
            hot = hot.astype(jnp.float32).astype(jnp.bfloat16)
            for pair in range(PAIRS):
                columns = slice(pair * PAIR, (pair + 1) * PAIR)
                if part == 0:
                    k, v = block[1, :, columns], block[2, :, columns]
                else:
                    other = others[slot // 2]
                    k, v = other[slot % 2, 0, :, columns], other[slot % 2, 1, :, columns]
                keys_new[2 * pair, rows, :] = jnp.where(low, k, hot)
                keys_new[2 * pair + 1, rows, :] = jnp.where(low, hot, k)
                values_new[columns, rows] = v.T
        first = slot % 2 * TILE
        for number in range(2 * PAIRS):
            bias = bias_ref[number, pl.ds(2 * chip + core, 1), :]
            bias = jnp.broadcast_to(bias, (TILE, PAIR)).astype(jnp.bfloat16)
            q = block[0, :, number // 2 * PAIR : (number // 2 + 1) * PAIR]
            q = jnp.where(low, q, bias) if number % 2 == 0 else jnp.where(low, bias, q)
            queries_new[number, first : first + TILE, :] = q

    keys = [group[0] for group in old + made]
    values = [group[1] for group in old + made]
    queries = [group[2] for group in old + made]

    every = tuple(range(seen + len(new)))
    items = [(head, [(u, new) for u in range(seen)] + [(u, every) for u in new]) for head in range(2)]

    def chunks(item):
        return [(u, group, part) for u, groups in item[1] for group in groups for part in range(KB // CK)]

    def score_chunk(pair, index, place, tops):
        head = items[index][0]
        u, group, part = chunks(items[index])[place]
        number = 2 * pair + head
        s = matmul(keys[group][number, part * CK : (part + 1) * CK, :], queries[u][number], ((1,), (1,)))
        scores[index % 2][place * CK : (place + 1) * CK, :] = s
        top = jnp.max(s.reshape(CK // 8, 8, QB), axis=0)
        return {**tops, u: jnp.maximum(tops[u], top) if u in tops else top}

    def one_pair(pair, tops, ends=False):
        finished = {}
        columns = pl.ds(pl.multiple_of(pair * PAIR, PAIR), PAIR)
        for index, item in enumerate(items):
            head = item[0]
            dims = pl.ds(pl.multiple_of(pair * PAIR + 64 * head, 64), 64)
            row_top, total, mixed = {}, {}, {}
            for u, _ in item[1]:
                row_top[u] = jnp.max(tops[u], axis=0, keepdims=True)
                total[u] = jnp.zeros((8, QB), jnp.float32)
                mixed[u] = jnp.zeros((64, QB), jnp.float32)
                if u < seen:
                    before = old[u][3][pair, head : head + 1, :]
                    row_top[u] = jnp.maximum(row_top[u], before)
                    fade = jnp.exp2((before - row_top[u]) * SCALE)
                    mixed[u] = old[u][4][dims, :] * fade
                    faded = old[u][3][pair, 8 + head : 9 + head, :] * fade
                    total[u] = jnp.where(lax.broadcasted_iota(jnp.int32, (8, QB), 0) == 0, faded, 0.0)
            now = chunks(item)
            following = (index + 1) % len(items)
            next_pair = pair if following else pair + 1
            later = 0 if ends and not following else len(chunks(items[following]))
            tops = {}
            done = 0
            for place, (u, group, part) in enumerate(now):
                until = (place + 1) * later // len(now)
                while done < until:
                    tops = score_chunk(next_pair, following, done, tops)
                    done += 1
                s = scores[index % 2][place * CK : (place + 1) * CK, :]
                weights = jnp.exp2((s - row_top[u]) * SCALE)
                total[u] = total[u] + jnp.sum(weights.reshape(CK // 8, 8, QB), axis=0)
                mixed[u] = mixed[u] + matmul(
                    values[group][dims, part * CK : (part + 1) * CK], weights.astype(jnp.bfloat16), ((1,), (0,))
                )
            for u, _ in item[1]:
                total[u] = jnp.sum(total[u], axis=0, keepdims=True)
                if not last:
                    new_state[u][0][pair, head : head + 1, :] = row_top[u]
                    new_state[u][0][pair, 8 + head : 9 + head, :] = total[u]
                    new_state[u][1][dims, :] = mixed[u]
                    continue
                finished[u, head] = mixed[u] / total[u]
                if head == 1:
                    query = lax.broadcasted_iota(jnp.int32, (1, QB), 1)
                    two = chips[2 * u : 2 * u + 2]
                    chip = jnp.where(query < TILE, two[0], two[1])
                    live = (2 * chip + core) * TILE + (query & (TILE - 1)) < length
                    both = jnp.concatenate([finished[u, 0], finished[u, 1]], axis=0)
                    both = jnp.where(live, both, 0.0).T.astype(jnp.bfloat16)
                    out_ref[two[0], :, columns] = both[:TILE]
                    out_ref[two[1], :, columns] = both[TILE:]
        return tops

    tops = {}
    for place in range(len(chunks(items[0]))):
        tops = score_chunk(0, 0, place, tops)
    tops = lax.fori_loop(0, PAIRS - 1, one_pair, tops)
    one_pair(PAIRS - 1, tops, ends=True)


def attend_wave(wave, lengths, masks, blocks, others, old):
    last = wave == len(WAVES) - 1
    new = WAVES[wave]
    bf16, f32 = jnp.bfloat16, jnp.float32
    kept = [((2 * PAIRS, KB, PAIR), bf16), ((WIDTH, KB), bf16), ((2 * PAIRS, QB, PAIR), bf16)] * len(new)
    groups = new[0] + len(new)
    made = [((2 * PAIRS, 16, PAIR), f32)] if wave == 0 else []
    made += kept + [((PAIRS, 16, QB), f32), ((WIDTH, QB), f32)] * groups
    operands = (lengths, *masks, *blocks, *others, *[array for group in old for array in group])
    scratch = [pltpu.VMEM(((new[0] * len(new) + len(new) * groups) * KB, QB), f32)] * 2
    if last:
        out_shape = jax.ShapeDtypeStruct((CHIPS, TILE, WIDTH), bf16)
        scratch = [pltpu.VMEM(*array) for array in made[: len(made) - 2 * groups]] + scratch
        out_specs = pl.BlockSpec(memory_space=pltpu.VMEM)
    else:
        out_shape = [jax.ShapeDtypeStruct(*array) for array in made]
        out_specs = [pl.BlockSpec(memory_space=pltpu.VMEM)] * len(out_shape)
    out = pl.pallas_call(
        functools.partial(wave_kernel, wave),
        out_shape=out_shape,
        in_specs=[pl.BlockSpec(memory_space=pltpu.SMEM)]
        + [pl.BlockSpec(memory_space=pltpu.VMEM)] * (len(operands) - 1),
        out_specs=out_specs,
        scratch_shapes=scratch,
        compiler_params=pltpu.CompilerParams(vmem_limit_bytes=32 * 2**20),
        cost_estimate=pl.CostEstimate(flops=0, bytes_accessed=0, transcendentals=0),
    )(*operands)
    if last:
        return out
    if wave == 0:
        masks, out = out[:1], out[1:]
    kept, states = out[: 3 * len(new)], out[3 * len(new) :]
    parts = [group[:3] for group in old] + [kept[3 * i : 3 * i + 3] for i in range(len(new))]
    return masks, [(*part, *states[2 * u : 2 * u + 2]) for u, part in enumerate(parts)]


def split_kernel(slots, q_ref, k_ref, v_ref, *refs):
    _, chips, _ = whereabouts()
    blocks, done = refs[:-1], refs[-1]
    copies = []
    for slot, block in zip(slots, blocks):
        columns = pl.ds(pl.multiple_of(chips[slot] * WIDTH, PAIR), WIDTH)
        for which, array in enumerate((q_ref, k_ref, v_ref)):
            copies.append(pltpu.make_async_copy(array.at[0, :, columns], block.at[which], done.at[len(copies)]))
    for copy in copies:
        copy.start()
    for copy in copies:
        copy.wait()


def split_columns(slots, *arrays):
    return pl.pallas_call(
        functools.partial(split_kernel, slots),
        out_shape=[jax.ShapeDtypeStruct((3, TILE, WIDTH), jnp.bfloat16)] * len(slots),
        in_specs=[pl.BlockSpec(memory_space=pl.ANY)] * 3,
        out_specs=[pl.BlockSpec(memory_space=pltpu.VMEM)] * len(slots),
        scratch_shapes=[pltpu.SemaphoreType.DMA((3 * len(slots),))],
    )(*arrays)


def join_kernel(blocks_ref, rows_ref, done):
    copies = [
        pltpu.make_async_copy(
            blocks_ref.at[chip], rows_ref.at[0, :, pl.ds(chip * WIDTH, WIDTH)], done.at[chip]
        )
        for chip in range(CHIPS)
    ]
    for copy in copies:
        copy.start()
    for copy in copies:
        copy.wait()


def join_columns(blocks):
    return pl.pallas_call(
        join_kernel,
        out_shape=jax.ShapeDtypeStruct((1, TILE, CHIPS * WIDTH), jnp.bfloat16),
        in_specs=[pl.BlockSpec(memory_space=pltpu.VMEM)],
        out_specs=pl.BlockSpec(memory_space=pl.ANY),
        scratch_shapes=[pltpu.SemaphoreType.DMA((CHIPS,))],
    )(blocks)


def after(array, earlier):
    return lax.optimization_barrier((array, earlier))[0]


def on_device(queries, key_states, value_states, clip_lengths, tile_masks):
    masks = tile_masks, lax.ppermute(tile_masks, "seq", OTHER_CORE)
    sent = [None] * CHIPS
    for slots in SPLITS:
        for slot, block in zip(slots, split_columns(slots, queries, key_states, value_states)):
            sent[slot] = block
    blocks = [sent[0]]
    for slot in range(1, CHIPS):
        blocks.append(lax.ppermute(sent[slot], "seq", route(*AWAY[slot])))

    groups = []
    for wave, new in enumerate(WAVES):
        now = blocks[2 * new[0] : 2 * new[-1] + 2]
        if wave > 0:
            now = after(now, groups[0][3])
        others = [
            lax.ppermute(jnp.stack([block[1:] for block in now[i : i + 2]]), "seq", OTHER_CORE)
            for i in range(0, len(now), 2)
        ]
        out = attend_wave(wave, clip_lengths, masks, now, others, groups)
        if wave < len(WAVES) - 1:
            masks, groups = out

    every = [[2 * chip + core for chip in range(CHIPS)] for core in range(2)]
    back = lax.all_to_all(out, "seq", 0, 0, tiled=True, axis_index_groups=every)
    return join_columns(back)


def solution(mesh):
    split = P("clip", "seq", None)
    return jax.shard_map(
        on_device,
        mesh=mesh,
        in_specs=(split, split, split, P(), P("clip", "seq", None, None)),
        out_specs=split,
        check_vma=False,
    )
```
